512 devices in a mesh: inp: 16 (over z), wgt: 8 (over y_hi, x), out: 4 (over y_lo, core).
Axes of the slice: x: 4, y: 4 (y_hi: 2, y_lo: 2; y = y_hi * 2 + y_lo), z: 16, core: 2. Of those that a mesh axis runs over, the one named last changes fastest.
Arguments:
- tokens: bfloat16 [256, 12288], P(('inp', 'out'), 'wgt'), may hold values from -6 to 6
- in_weight: bfloat16 [12288, 24576], P('wgt', ('inp', 'out')), may hold values from -0.0546875 to 0.0546875
- out_weight: bfloat16 [24576, 12288], P(('inp', 'out'), 'wgt'), may hold values from -0.0390625 to 0.0390625
- grad_output: bfloat16 [256, 12288], P(('inp', 'out'), 'wgt'), may hold values from -3 to 3
Outputs:
- result: bfloat16 [256, 12288], P(('inp', 'out'), 'wgt')
- grad_tokens: bfloat16 [256, 12288], P(('inp', 'out'), 'wgt')
- grad_in_weight: bfloat16 [12288, 24576], P('wgt', ('inp', 'out'))
- grad_out_weight: bfloat16 [24576, 12288], P(('inp', 'out'), 'wgt')
The draws below stay inside these ranges and needn't reach their ends.
All inputs are finite; a program needn't handle non-finite values.
Results may differ from the reference program's by a relative error of at most 0.024.
Values may be sent and summed in bfloat16 or wider, within the bound.
A program may use at most 64 MiB of HBM per device.

```python
import math
import jax
import jax.numpy as jnp
from jax import lax

D = 12288
F = 24576
TOKENS = 256


def steps_of(key, dims, pieces, low, high):
    def one(position, parts):
        draws = jax.random.uniform(jax.random.fold_in(jax.random.fold_in(key, 6), position), (parts,), jnp.float32, low / len(pieces), high / len(pieces))
        return jnp.repeat(jnp.exp(draws), dims[position] // parts).reshape((-1,) + (1,) * (len(dims) - position - 1))

    factor_of = one(*pieces[0])
    for cut in pieces[1:]:
        factor_of = factor_of * one(*cut)
    return factor_of


def normal_values(own_key, shape, width, limit, cuts=(), held_as=jnp.bfloat16):
    values = width * jax.random.normal(own_key, shape, jnp.float32)
    if cuts:
        values = values * steps_of(own_key, shape, cuts, -0.22, 0.18)
    return jnp.clip(values, -limit, limit).astype(held_as)


def setup_inputs(seed: int = 0) -> dict:
    key_of = jax.random.split(jax.random.key(seed), 5)
    return {
        "tokens": normal_values(key_of[0], (TOKENS, D), 1.0, 6.0, ((0, 64), (1, 8))),
        "in_weight": normal_values(key_of[1], (D, F), D ** -0.5, 0.0546875, ((0, 8), (1, 64))),
        "out_weight": normal_values(key_of[2], (F, D), F ** -0.5, 0.0390625, ((0, 64), (1, 8))),
        "grad_output": normal_values(key_of[3], (TOKENS, D), 0.5, 3.0, ((0, 64), (1, 8))),
    }


gelu_c = math.sqrt(2.0 / math.pi)

def gelu_value(v):
    inner = jnp.tanh(gelu_c * (v + 0.044715 * v * v * v))
    return 0.5 * v * (1.0 + inner)

def gelu_slope(v):
    inner = jnp.tanh(gelu_c * (v + 0.044715 * v * v * v))
    return 0.5 * (1.0 + inner) + 0.5 * v * (1.0 - inner * inner) * gelu_c * (1.0 + 3.0 * 0.044715 * v * v)

def reference(tokens, in_weight, out_weight, grad_output):
    preact = jnp.dot(tokens, in_weight, preferred_element_type=jnp.float32)
    hidden = gelu_value(preact).astype(jnp.bfloat16)
    result = jnp.dot(hidden, out_weight, preferred_element_type=jnp.float32).astype(jnp.bfloat16)
    grad_hidden = lax.dot_general(grad_output, out_weight, (((1,), (1,)), ((), ())), preferred_element_type=jnp.float32)
    grad_preact = (grad_hidden * gelu_slope(preact)).astype(jnp.bfloat16)
    grad_tokens = lax.dot_general(grad_preact, in_weight, (((1,), (1,)), ((), ())), preferred_element_type=jnp.float32).astype(jnp.bfloat16)
    grad_in_weight = lax.dot_general(tokens, grad_preact, (((0,), (0,)), ((), ())), preferred_element_type=jnp.float32).astype(jnp.bfloat16)
    grad_out_weight = lax.dot_general(hidden, grad_output, (((0,), (0,)), ((), ())), preferred_element_type=jnp.float32).astype(jnp.bfloat16)
    return (result, grad_tokens, grad_in_weight, grad_out_weight)
```

```python
import math

import jax
import jax.numpy as jnp
from jax import lax
from jax.experimental import pallas as pl
from jax.experimental.pallas import tpu as pltpu
from jax.sharding import PartitionSpec as P

MESH = pl.DeviceIdType.MESH
f32 = jnp.float32
bf16 = jnp.bfloat16

gelu_c = math.sqrt(2.0 / math.pi)

FAR = (-6, -2, 2, 6)
NEAR = ((0, 0), (1, 0), (-1, 0), (2, 0), (0, 1), (1, 1), (-1, 1), (-2, 1))
NEAR_ORDER = (7, 5, 6, 3, 4, 1, 2)
PEERS = ((2, 1), (1, 1), (3, 1), (2, 0), (0, 1), (1, 0), (3, 0))


def gelu_value_and_slope(v):
    inner = jnp.tanh(gelu_c * (v + 0.044715 * v * v * v))
    value = 0.5 * v * (1.0 + inner)
    slope = 0.5 * (1.0 + inner) + 0.5 * v * (1.0 - inner * inner) * gelu_c * (
        1.0 + 3.0 * 0.044715 * v * v
    )
    return value, slope


def kernel(
    tok_ref, w1_hbm, w2_hbm, cot_ref,
    res_ref, gt_ref, giw_hbm, gow_hbm,
    w1, w2, giw, gow,
    own, farbuf, stage, rows, part, recva, act, slope,
    keep, sibsend, sibrecv, nearsend, nearrecv, farsend, farrecv,
    load_sem, store_sem,
    far_s, far_r, near_s, near_r, sib_s, sib_r, pa_s, pa_r, pb_s, pb_r,
    rsib_s, rsib_r, rnear_s, rnear_r, rfar_s, rfar_r,
):
    z = lax.axis_index("inp")
    w = lax.axis_index("wgt")
    o = lax.axis_index("out")
    x = w % 4
    yh = w // 4

    def at_z(dz, dy=0):
        return ((z + dz + 16) % 16, w, (o + 2 * dy) % 4)

    sibling = (z, w, o + 1 - 2 * (o % 2))

    def peer_index(k):
        dx, dy = PEERS[k]
        return ((yh + dy) % 2) * 4 + (x + dx) % 4

    load1 = pltpu.make_async_copy(w1_hbm, w1, load_sem.at[0])
    load2 = pltpu.make_async_copy(w2_hbm, w2, load_sem.at[1])
    load1.start()
    load2.start()

    barrier = pltpu.get_barrier_semaphore()
    partners = [at_z(d) for d in (6, -6, 2, -2, 1, -1)]
    partners += [at_z(d, 1) for d in (2, -2, 1, -1, 0)]
    partners += [(z, peer_index(k), o) for k in range(7)]
    partners += [sibling]
    for partner in partners:
        pl.semaphore_signal(barrier, inc=1, device_id=partner, device_id_type=MESH)
    own[0] = tok_ref[...]
    own[1] = cot_ref[...]
    pl.semaphore_wait(barrier, len(partners))

    def remote(src, dst, send, recv, device):
        return pltpu.make_async_remote_copy(
            src_ref=src, dst_ref=dst, send_sem=send, recv_sem=recv,
            device_id=device, device_id_type=MESH,
        )

    def far_copy(t, j):
        return remote(own.at[t], farbuf.at[t, j], far_s.at[t, j], far_r.at[t, j], at_z(-FAR[j]))

    def near_copy(t, m):
        dz, dy = NEAR[m]
        return remote(
            rows.at[t, 0, 0], rows.at[t, 0, m], near_s.at[t, m], near_r.at[t, m], at_z(-dz, dy)
        )

    def sib_copy(t, m):
        return remote(rows.at[t, 0, m], rows.at[t, 1, m], sib_s.at[t, m], sib_r.at[t, m], sibling)

    def pa_copy(t, k):
        p = peer_index(k)
        return remote(part.at[t, p], recva.at[t, k], pa_s.at[t, k], pa_r.at[t, k], (z, p, o))

    def pb_copy(t, k):
        return remote(
            act.at[t, w], act.at[t, w], pb_s.at[t, k], pb_r.at[t, k], (z, peer_index(k), o)
        )

    def rsib_copy(t, m):
        return remote(
            sibsend.at[t, m], sibrecv.at[t, m], rsib_s.at[t, m], rsib_r.at[t, m], sibling
        )

    def rnear_copy(t, m):
        dz, dy = NEAR[m]
        return remote(
            nearsend.at[t, m], nearrecv.at[t, m], rnear_s.at[t, m], rnear_r.at[t, m], at_z(dz, dy)
        )

    def rfar_copy(t, j):
        return remote(
            farsend.at[t, j], farrecv.at[t, j], rfar_s.at[t, j], rfar_r.at[t, j], at_z(FAR[j])
        )

    for t in range(2):
        for j in (0, 3, 1, 2):
            far_copy(t, j).start()
    for t in range(2):
        for j in (1, 2, 0, 3):
            far_copy(t, j).wait_recv()
            stage[t, 4 * j : 4 * j + 4, :] = farbuf[t, j].astype(f32)
        rows[t, 0, 0] = stage[t].astype(bf16)
        for m in NEAR_ORDER:
            near_copy(t, m).start()
        sib_copy(t, 0).start()

    for t in range(2):
        for m in reversed(NEAR_ORDER):
            near_copy(t, m).wait_recv()
            sib_copy(t, m).start()
        for m in range(8):
            sib_copy(t, m).wait_recv()
        (load1, load2)[t].wait()
        gathered = rows[t].reshape(256, 1536)
        if t == 0:
            product = jnp.dot(gathered, w1[...], preferred_element_type=f32)
        else:
            product = lax.dot_general(
                gathered, w2[...], (((1,), (1,)), ((), ())), preferred_element_type=f32
            )
        part[t] = product.astype(bf16).reshape(8, 32, 384)
        for k in range(7):
            pa_copy(t, k).start()

    for t in range(2):
        total = part[t, w].astype(f32)
        for k in reversed(range(7)):
            pa_copy(t, k).wait_recv()
            total = total + recva[t, k].astype(f32)
        if t == 0:
            value, slope_value = gelu_value_and_slope(total)
            slope[...] = slope_value
        else:
            value = total * slope[...]
        act[t, w] = value.astype(bf16)
        for k in range(7):
            pb_copy(t, k).start()

    for t in range(2):
        for k in reversed(range(7)):
            pb_copy(t, k).wait_recv()
        block = act.at[t]

        def column_tile(i, carry, t=t, block=block):
            at = pl.ds(pl.multiple_of(i * 256, 256), 256)
            left = block[...].reshape(256, 384)
            if t == 0:
                product = jnp.dot(left, w2[:, at], preferred_element_type=f32)
            else:
                product = lax.dot_general(
                    left, w1[at, :], (((1,), (1,)), ((), ())), preferred_element_type=f32
                )
            keep[t, :, :, at] = product[:128].reshape(8, 16, 256)
            sibsend[t, :, :, at] = product[128:].astype(bf16).reshape(8, 16, 256)
            return carry

        lax.fori_loop(0, 6, column_tile, 0)
        for m in NEAR_ORDER + (0,):
            rsib_copy(t, m).start()
        for m in NEAR_ORDER:
            rsib_copy(t, m).wait_recv()
            nearsend[t, m] = (keep[t, m] + sibrecv[t, m].astype(f32)).astype(bf16)
            rnear_copy(t, m).start()

    def gow_tile(i, carry):
        at = pl.ds(pl.multiple_of(i * 256, 256), 256)
        right = rows[1, :, :, :, at].reshape(256, 256)
        gow[:, at] = lax.dot_general(
            act[0].reshape(256, 384), right, (((0,), (0,)), ((), ())), preferred_element_type=f32
        ).astype(bf16)
        return carry

    lax.fori_loop(0, 6, gow_tile, 0)
    store2 = pltpu.make_async_copy(gow, gow_hbm, store_sem.at[1])
    store2.start()

    def giw_tile(i, carry):
        at = pl.ds(pl.multiple_of(i * 256, 256), 256)
        left = rows[0, :, :, :, at].reshape(256, 256)
        giw[at, :] = lax.dot_general(
            left, act[1].reshape(256, 384), (((0,), (0,)), ((), ())), preferred_element_type=f32
        ).astype(bf16)
        return carry

    lax.fori_loop(0, 6, giw_tile, 0)
    store1 = pltpu.make_async_copy(giw, giw_hbm, store_sem.at[0])
    store1.start()

    for t in range(2):
        rsib_copy(t, 0).wait_recv()
        total = keep[t, 0] + sibrecv[t, 0].astype(f32)
        for m in reversed(NEAR_ORDER):
            rnear_copy(t, m).wait_recv()
            total = total + nearrecv[t, m].astype(f32)
        stage[t] = total
        for j in (0, 3, 1, 2):
            farsend[t, j] = stage[t, 4 * j : 4 * j + 4, :].astype(bf16)
            rfar_copy(t, j).start()
    for t in range(2):
        total = jnp.zeros((4, 1536), f32)
        for j in (1, 2, 0, 3):
            rfar_copy(t, j).wait_recv()
            total = total + farrecv[t, j].astype(f32)
        (res_ref, gt_ref)[t][...] = total.astype(bf16)

    for t in range(2):
        for j in range(4):
            far_copy(t, j).wait_send()
            rfar_copy(t, j).wait_send()
        for m in NEAR_ORDER:
            near_copy(t, m).wait_send()
            rnear_copy(t, m).wait_send()
        for m in range(8):
            sib_copy(t, m).wait_send()
            rsib_copy(t, m).wait_send()
        for k in range(7):
            pa_copy(t, k).wait_send()
            pb_copy(t, k).wait_send()
    store2.wait()
    store1.wait()


def on_device(tokens, in_weight, out_weight, grad_output):
    vmem = pl.BlockSpec(memory_space=pltpu.VMEM)
    hbm = pl.BlockSpec(memory_space=pl.ANY)
    dma = pltpu.SemaphoreType.DMA
    return pl.pallas_call(
        kernel,
        out_shape=(
            jax.ShapeDtypeStruct((4, 1536), bf16),
            jax.ShapeDtypeStruct((4, 1536), bf16),
            jax.ShapeDtypeStruct((1536, 384), bf16),
            jax.ShapeDtypeStruct((384, 1536), bf16),
        ),
        in_specs=[vmem, hbm, hbm, vmem],
        out_specs=(vmem, vmem, hbm, hbm),
        scratch_shapes=[
            pltpu.VMEM((1536, 384), bf16),
            pltpu.VMEM((384, 1536), bf16),
            pltpu.VMEM((1536, 384), bf16),
            pltpu.VMEM((384, 1536), bf16),
            pltpu.VMEM((2, 4, 1536), bf16),
            pltpu.VMEM((2, 4, 4, 1536), bf16),
            pltpu.VMEM((2, 16, 1536), f32),
            pltpu.VMEM((2, 2, 8, 16, 1536), bf16),
            pltpu.VMEM((2, 8, 32, 384), bf16),
            pltpu.VMEM((2, 7, 32, 384), bf16),
            pltpu.VMEM((2, 8, 32, 384), bf16),
            pltpu.VMEM((32, 384), f32),
            pltpu.VMEM((2, 8, 16, 1536), f32),
            pltpu.VMEM((2, 8, 16, 1536), bf16),
            pltpu.VMEM((2, 8, 16, 1536), bf16),
            pltpu.VMEM((2, 8, 16, 1536), bf16),
            pltpu.VMEM((2, 8, 16, 1536), bf16),
            pltpu.VMEM((2, 4, 4, 1536), bf16),
            pltpu.VMEM((2, 4, 4, 1536), bf16),
            dma((2,)),
            dma((2,)),
        ]
        + [dma((2, n)) for n in (4, 4, 8, 8, 8, 8, 7, 7, 7, 7, 8, 8, 8, 8, 4, 4)],
        compiler_params=pltpu.CompilerParams(
            collective_id=0, has_side_effects=True, vmem_limit_bytes=40 * 2**20
        ),
        cost_estimate=pl.CostEstimate(
            flops=12 * 256 * 1536 * 384, bytes_accessed=4 * 1536 * 384 * 2, transcendentals=32 * 384
        ),
    )(tokens, in_weight, out_weight, grad_output)


def solution(mesh):
    in_specs = (
        P(("inp", "out"), "wgt"),
        P("wgt", ("inp", "out")),
        P(("inp", "out"), "wgt"),
        P(("inp", "out"), "wgt"),
    )
    out_specs = (
        P(("inp", "out"), "wgt"),
        P(("inp", "out"), "wgt"),
        P("wgt", ("inp", "out")),
        P(("inp", "out"), "wgt"),
    )
    return jax.shard_map(
        on_device, mesh=mesh, in_specs=in_specs, out_specs=out_specs, check_vma=False
    )
```

```python
import math

import jax
import jax.numpy as jnp
from jax import lax
from jax.experimental import pallas as pl
from jax.experimental.pallas import tpu as pltpu
from jax.sharding import PartitionSpec as P

MESH = pl.DeviceIdType.MESH
f32 = jnp.float32
bf16 = jnp.bfloat16

gelu_c = math.sqrt(2.0 / math.pi)

FAR = (-6, -2, 2, 6)
NEAR = ((0, 0), (1, 0), (-1, 0), (2, 0), (0, 1), (1, 1), (-1, 1), (-2, 1))
NEAR_ORDER = (7, 5, 6, 3, 4, 1, 2)
PEERS = ((2, 1), (1, 1), (3, 1), (2, 0), (0, 1), (1, 0), (3, 0))


def gelu_value_and_slope(v):
    inner = jnp.tanh(gelu_c * (v + 0.044715 * v * v * v))
    value = 0.5 * v * (1.0 + inner)
    slope = 0.5 * (1.0 + inner) + 0.5 * v * (1.0 - inner * inner) * gelu_c * (
        1.0 + 3.0 * 0.044715 * v * v
    )
    return value, slope


def kernel(
    tok_hbm, w1_hbm, w2_hbm, cot_hbm,
    res_ref, gt_ref, giw, gow,
    w1, w2, w1t, w2t,
    own, farbuf, stage, rows, part, recva, act, shared, slope,
    keep, nearsend, nearrecv, farsend, farrecv,
    load_sem, weight_s, weight_r, rows_s, rows_r, shared_s, shared_r,
    far_s, far_r, near_s, near_r, pa_s, pa_r, pb_s, pb_r,
    rnear_s, rnear_r, rfar_s, rfar_r,
):
    z = lax.axis_index("inp")
    w = lax.axis_index("wgt")
    o = lax.axis_index("out")
    x = w % 4
    yh = w // 4

    def at_z(dz, dy=0):
        return ((z + dz + 16) % 16, w, (o + 2 * dy) % 4)

    sibling = (z, w, o + 1 - 2 * (o % 2))

    def peer_index(k):
        dx, dy = PEERS[k]
        return ((yh + dy) % 2) * 4 + (x + dx) % 4

    loads = [
        pltpu.make_async_copy(src, dst, load_sem.at[i])
        for i, (src, dst) in enumerate(
            (
                (tok_hbm, own.at[0]),
                (cot_hbm, own.at[1]),
                (w2_hbm, w2.at[pl.ds(0, 384)]),
                (w1_hbm, w1.at[:, pl.ds(0, 384)]),
            )
        )
    ]
    for load in loads:
        load.start()

    barrier = pltpu.get_barrier_semaphore()
    partners = [at_z(d) for d in (6, -6, 2, -2, 1, -1)]
    partners += [at_z(d, 1) for d in (2, -2, 1, -1, 0)]
    partners += [(z, peer_index(k), o) for k in range(7)]
    partners += [sibling]
    for partner in partners:
        pl.semaphore_signal(barrier, inc=1, device_id=partner, device_id_type=MESH)
    loads[0].wait()
    loads[1].wait()
    pl.semaphore_wait(barrier, len(partners))

    def remote(src, dst, send, recv, device):
        return pltpu.make_async_remote_copy(
            src_ref=src, dst_ref=dst, send_sem=send, recv_sem=recv,
            device_id=device, device_id_type=MESH,
        )

    sent = []

    def start(copy):
        copy.start()
        sent.append(copy)

    def far_copy(t, j):
        return remote(own.at[t], farbuf.at[t, j], far_s.at[t, j], far_r.at[t, j], at_z(-FAR[j]))

    def near_copy(t, m):
        dz, dy = NEAR[m]
        return remote(
            rows.at[t, 0, 0], rows.at[t, 0, m], near_s.at[t, m], near_r.at[t, m], at_z(-dz, dy)
        )

    def rows_copy(t):
        return remote(rows.at[t, 0], rows.at[t, 1], rows_s.at[t], rows_r.at[t], sibling)

    def shared_copy(t):
        return remote(
            act.at[t, :, :, pl.ds(384, 384)], shared.at[t, 1], shared_s.at[t], shared_r.at[t],
            sibling,
        )

    def pa_copy(t, k):
        p = peer_index(k)
        return remote(part.at[t, p], recva.at[t, k], pa_s.at[t, k], pa_r.at[t, k], (z, p, o))

    def pb_copy(t, k):
        return remote(
            act.at[t, w], act.at[t, w], pb_s.at[t, k], pb_r.at[t, k], (z, peer_index(k), o)
        )

    def rnear_copy(t, m):
        dz, dy = NEAR[m]
        return remote(
            nearsend.at[t, m], nearrecv.at[t, m], rnear_s.at[t, m], rnear_r.at[t, m], at_z(dz, dy)
        )

    def rfar_copy(t, j):
        return remote(
            farsend.at[t, j], farrecv.at[t, j], rfar_s.at[t, j], rfar_r.at[t, j], at_z(FAR[j])
        )

    for t in range(2):
        for j in (0, 3, 1, 2):
            start(far_copy(t, j))
    weights = (
        remote(w2_hbm, w2.at[pl.ds(384, 384)], weight_s.at[0], weight_r.at[0], sibling),
        remote(w1_hbm, w1.at[:, pl.ds(384, 384)], weight_s.at[1], weight_r.at[1], sibling),
    )
    for copy in weights:
        start(copy)
    loads[2].wait()
    weights[0].wait_recv()
    w2t[...] = w2[...].T
    for t in range(2):
        for j in (1, 2, 0, 3):
            far_copy(t, j).wait_recv()
            stage[t, 4 * j : 4 * j + 4, :] = farbuf[t, j].astype(f32)
        rows[t, 0, 0] = stage[t].astype(bf16)
        for m in NEAR_ORDER:
            start(near_copy(t, m))
    loads[3].wait()
    weights[1].wait_recv()
    w1t[...] = w1[...].T

    for t in range(2):
        for m in reversed(NEAR_ORDER):
            near_copy(t, m).wait_recv()
        part[t] = (
            jnp.dot(
                rows[t, 0].reshape(128, 1536), (w1, w2t)[t][...], preferred_element_type=f32
            )
            .astype(bf16)
            .reshape(8, 16, 768)
        )
        for k in range(7):
            start(pa_copy(t, k))
        start(rows_copy(t))

    for t in range(2):
        total = part[t, w].astype(f32)
        for k in reversed(range(7)):
            pa_copy(t, k).wait_recv()
            total = total + recva[t, k].astype(f32)
        if t == 0:
            value, slope_value = gelu_value_and_slope(total)
            slope[...] = slope_value
        else:
            value = total * slope[...]
        act[t, w] = value.astype(bf16)
        for k in range(7):
            start(pb_copy(t, k))

    for t in range(2):
        for k in reversed(range(7)):
            pb_copy(t, k).wait_recv()
        product = jnp.dot(
            act[t].reshape(128, 768), (w2, w1t)[t][...], preferred_element_type=f32
        ).reshape(8, 16, 1536)
        nearsend[t] = product.astype(bf16)
        keep[t] = product[0]
        for m in NEAR_ORDER:
            start(rnear_copy(t, m))
        start(shared_copy(t))
        shared[t, 0] = act[t, :, :, :384]

    for t in range(2):
        rows_copy(1 - t).wait_recv()
        shared_copy(t).wait_recv()
        units = shared[t].reshape(256, 384)
        other = rows[1 - t].reshape(256, 1536)
        if t == 0:
            gow[...] = lax.dot_general(
                units, other, (((0,), (0,)), ((), ())), preferred_element_type=f32
            ).astype(bf16)
        else:
            giw[...] = lax.dot_general(
                other, units, (((0,), (0,)), ((), ())), preferred_element_type=f32
            ).astype(bf16)

    for t in range(2):
        total = keep[t]
        for m in reversed(NEAR_ORDER):
            rnear_copy(t, m).wait_recv()
            total = total + nearrecv[t, m].astype(f32)
        stage[t] = total
        for j in (0, 3, 1, 2):
            farsend[t, j] = stage[t, 4 * j : 4 * j + 4, :].astype(bf16)
            start(rfar_copy(t, j))
    for t in range(2):
        total = jnp.zeros((4, 1536), f32)
        for j in (1, 2, 0, 3):
            rfar_copy(t, j).wait_recv()
            total = total + farrecv[t, j].astype(f32)
        (res_ref, gt_ref)[t][...] = total.astype(bf16)

    for copy in sent:
        copy.wait_send()


def store_kernel(*refs):
    sem = refs[8]
    stores = [pltpu.make_async_copy(refs[i], refs[4 + i], sem.at[i]) for i in (2, 3, 0, 1)]
    for store in stores:
        store.start()
    for store in stores:
        store.wait()


def on_device(*arguments):
    vmem = pl.BlockSpec(memory_space=pltpu.VMEM)
    hbm = pl.BlockSpec(memory_space=pltpu.HBM)
    dma = pltpu.SemaphoreType.DMA
    out_shape = (
        jax.ShapeDtypeStruct((4, 1536), bf16),
        jax.ShapeDtypeStruct((4, 1536), bf16),
        jax.ShapeDtypeStruct((1536, 384), bf16),
        jax.ShapeDtypeStruct((384, 1536), bf16),
    )
    outputs = pl.pallas_call(
        kernel,
        out_shape=out_shape,
        in_specs=[hbm] * 4,
        out_specs=(vmem,) * 4,
        scratch_shapes=[
            pltpu.VMEM((1536, 768), bf16),
            pltpu.VMEM((768, 1536), bf16),
            pltpu.VMEM((768, 1536), bf16),
            pltpu.VMEM((1536, 768), bf16),
            pltpu.VMEM((2, 4, 1536), bf16),
            pltpu.VMEM((2, 4, 4, 1536), bf16),
            pltpu.VMEM((2, 16, 1536), f32),
            pltpu.VMEM((2, 2, 8, 16, 1536), bf16),
            pltpu.VMEM((2, 8, 16, 768), bf16),
            pltpu.VMEM((2, 7, 16, 768), bf16),
            pltpu.VMEM((2, 8, 16, 768), bf16),
            pltpu.VMEM((2, 2, 8, 16, 384), bf16),
            pltpu.VMEM((16, 768), f32),
            pltpu.VMEM((2, 16, 1536), f32),
            pltpu.VMEM((2, 8, 16, 1536), bf16),
            pltpu.VMEM((2, 8, 16, 1536), bf16),
            pltpu.VMEM((2, 4, 4, 1536), bf16),
            pltpu.VMEM((2, 4, 4, 1536), bf16),
            dma((4,)),
        ]
        + [dma((2,))] * 6
        + [dma((2, n)) for n in (4, 4, 8, 8, 7, 7, 7, 7, 8, 8, 4, 4)],
        compiler_params=pltpu.CompilerParams(
            collective_id=0, has_side_effects=True, vmem_limit_bytes=40 * 2**20
        ),
        cost_estimate=pl.CostEstimate(
            flops=12 * 256 * 1536 * 384, bytes_accessed=4 * 1536 * 384 * 2, transcendentals=32 * 384
        ),
    )(*(pltpu.with_memory_space_constraint(a, pltpu.HBM) for a in arguments))
    return pl.pallas_call(
        store_kernel,
        out_shape=out_shape,
        in_specs=[vmem] * 4,
        out_specs=(hbm,) * 4,
        scratch_shapes=[dma((4,))],
        compiler_params=pltpu.CompilerParams(vmem_limit_bytes=8 * 2**20),
    )(*outputs)


def solution(mesh):
    in_specs = (
        P(("inp", "out"), "wgt"),
        P("wgt", ("inp", "out")),
        P(("inp", "out"), "wgt"),
        P(("inp", "out"), "wgt"),
    )
    out_specs = (
        P(("inp", "out"), "wgt"),
        P(("inp", "out"), "wgt"),
        P("wgt", ("inp", "out")),
        P(("inp", "out"), "wgt"),
    )
    return jax.shard_map(
        on_device, mesh=mesh, in_specs=in_specs, out_specs=out_specs, check_vma=False
    )
```

```python
import math

import jax
import jax.numpy as jnp
from jax import lax
from jax.experimental import pallas as pl
from jax.experimental.pallas import tpu as pltpu
from jax.sharding import PartitionSpec as P

MESH = pl.DeviceIdType.MESH
f32 = jnp.float32
bf16 = jnp.bfloat16

gelu_c = math.sqrt(2.0 / math.pi)

FAR = (-2, -6, 6, 2)
FAR_ORDER = (1, 2, 0, 3)
NEAR = ((0, 0), (1, 0), (-1, 0), (2, 0), (0, 1), (1, 1), (-1, 1), (-2, 1))
NEAR_ORDER = (7, 5, 6, 3, 4, 1, 2)
SPAN = (None, (1, 4), (0, 3), (1, 4), (1, 3), (1, 4), (0, 3), (0, 3))
DIRECT = ((4, 0), (4, 3), (5, 0), (6, 3), (1, 0), (2, 3), (7, 3))
HOME = (3, 0)
PEERS = ((2, 1), (1, 1), (3, 1), (2, 0), (0, 1), (1, 0), (3, 0))


def gelu_value_and_slope(v):
    inner = jnp.tanh(gelu_c * (v + 0.044715 * v * v * v))
    value = 0.5 * v * (1.0 + inner)
    slope = 0.5 * (1.0 + inner) + 0.5 * v * (1.0 - inner * inner) * gelu_c * (
        1.0 + 3.0 * 0.044715 * v * v
    )
    return value, slope


def kernel(
    tok_hbm, w1_hbm, w2_hbm, cot_hbm,
    res_ref, gt_ref, giw, gow,
    w1, w2, w1t, w2t,
    own, blocks, stage, rows, part, recva, act, shared, slope,
    keep, back, nearrecv, directrecv, farsend, farrecv,
    load_sem, weight_s, weight_r, rows_s, rows_r, shared_s, shared_r,
    far_s, far_r, near_s, near_r, pa_s, pa_r, pb_s, pb_r,
    rnear_s, rnear_r, rfar_s, rfar_r, direct_s, direct_r, rdirect_s, rdirect_r,
):
    z = lax.axis_index("inp")
    w = lax.axis_index("wgt")
    o = lax.axis_index("out")
    x = w % 4
    yh = w // 4

    def at_z(dz, dy=0):
        return ((z + dz + 16) % 16, w, (o + 2 * dy) % 4)

    sibling = (z, w, o + 1 - 2 * (o % 2))

    def peer_index(k):
        dx, dy = PEERS[k]
        return ((yh + dy) % 2) * 4 + (x + dx) % 4

    loads = [
        pltpu.make_async_copy(src, dst, load_sem.at[i])
        for i, (src, dst) in enumerate(
            (
                (tok_hbm, own.at[0]),
                (cot_hbm, own.at[1]),
                (w2_hbm, w2.at[pl.ds(0, 384)]),
                (w1_hbm, w1.at[:, pl.ds(0, 384)]),
            )
        )
    ]
    for load in loads:
        load.start()

    barrier = pltpu.get_barrier_semaphore()
    partners = [at_z(d) for d in (6, -6, 2, -2, 1, -1)]
    partners += [at_z(d, 1) for d in (2, -2, 1, -1, 0)]
    partners += [(z, peer_index(k), o) for k in range(7)]
    partners += [sibling]
    for partner in partners:
        pl.semaphore_signal(barrier, inc=1, device_id=partner, device_id_type=MESH)
    loads[0].wait()
    loads[1].wait()
    pl.semaphore_wait(barrier, len(partners))

    def remote(src, dst, send, recv, device):
        return pltpu.make_async_remote_copy(
            src_ref=src, dst_ref=dst, send_sem=send, recv_sem=recv,
            device_id=device, device_id_type=MESH,
        )

    sent = []

    def start(copy):
        copy.start()
        sent.append(copy)

    def far_copy(t, j):
        return remote(own.at[t], blocks.at[t, 0, j], far_s.at[t, j], far_r.at[t, j], at_z(-FAR[j]))

    def direct_copy(t, i):
        m, j = DIRECT[i]
        dz, dy = NEAR[m]
        return remote(
            own.at[t], blocks.at[t, m, j], direct_s.at[t, i], direct_r.at[t, i],
            at_z(-dz - FAR[j], dy),
        )

    def near_copy(t, m):
        dz, dy = NEAR[m]
        span = pl.ds(SPAN[m][0], SPAN[m][1] - SPAN[m][0])
        return remote(
            blocks.at[t, 0, span], blocks.at[t, m, span], near_s.at[t, m], near_r.at[t, m],
            at_z(-dz, dy),
        )

    def rows_copy(t):
        return remote(rows.at[t, 0], rows.at[t, 1], rows_s.at[t], rows_r.at[t], sibling)

    def shared_copy(t):
        return remote(
            act.at[t, :, :, pl.ds(384, 384)], shared.at[t, 1], shared_s.at[t], shared_r.at[t],
            sibling,
        )

    def pa_copy(t, k):
        p = peer_index(k)
        return remote(part.at[t, p], recva.at[t, k], pa_s.at[t, k], pa_r.at[t, k], (z, p, o))

    def pb_copy(t, k):
        return remote(
            act.at[t, w], act.at[t, w], pb_s.at[t, k], pb_r.at[t, k], (z, peer_index(k), o)
        )

    def rdirect_copy(t, i):
        m, j = DIRECT[i]
        dz, dy = NEAR[m]
        return remote(
            back.at[t, m, j], directrecv.at[t, i], rdirect_s.at[t, i], rdirect_r.at[t, i],
            at_z(dz + FAR[j], dy),
        )

    def rnear_copy(t, m):
        dz, dy = NEAR[m]
        span = pl.ds(SPAN[m][0], SPAN[m][1] - SPAN[m][0])
        return remote(
            back.at[t, m, span], nearrecv.at[t, m, span], rnear_s.at[t, m], rnear_r.at[t, m],
            at_z(dz, dy),
        )

    def rfar_copy(t, j):
        return remote(
            farsend.at[t, j], farrecv.at[t, j], rfar_s.at[t, j], rfar_r.at[t, j], at_z(FAR[j])
        )

    for t in range(2):
        for j in FAR_ORDER:
            start(far_copy(t, j))
    for t in range(2):
        for i in range(7):
            start(direct_copy(t, i))
    weights = (
        remote(w2_hbm, w2.at[pl.ds(384, 384)], weight_s.at[0], weight_r.at[0], sibling),
        remote(w1_hbm, w1.at[:, pl.ds(384, 384)], weight_s.at[1], weight_r.at[1], sibling),
    )
    for copy in weights:
        start(copy)
    for t in range(2):
        blocks[t, HOME[0], HOME[1]] = own[t]
    loads[2].wait()
    weights[0].wait_recv()
    w2t[...] = w2[...].T

    def to_rows(t, m):
        for j in range(4):
            stage[t, 4 * j : 4 * j + 4, :] = blocks[t, m, j].astype(f32)
        rows[t, 0, m] = stage[t].astype(bf16)

    for t in range(2):
        for j in reversed(FAR_ORDER):
            far_copy(t, j).wait_recv()
        for m in NEAR_ORDER:
            start(near_copy(t, m))
        to_rows(t, 0)
    loads[3].wait()
    weights[1].wait_recv()
    w1t[...] = w1[...].T

    for t in range(2):
        for i in range(7):
            direct_copy(t, i).wait_recv()
        for m in reversed(NEAR_ORDER):
            near_copy(t, m).wait_recv()
            to_rows(t, m)
        part[t] = (
            jnp.dot(
                rows[t, 0].reshape(128, 1536), (w1, w2t)[t][...], preferred_element_type=f32
            )
            .astype(bf16)
            .reshape(8, 16, 768)
        )
        for k in range(7):
            start(pa_copy(t, k))
        start(rows_copy(t))

    for t in range(2):
        total = part[t, w].astype(f32)
        for k in reversed(range(7)):
            pa_copy(t, k).wait_recv()
            total = total + recva[t, k].astype(f32)
        if t == 0:
            value, slope_value = gelu_value_and_slope(total)
            slope[...] = slope_value
        else:
            value = total * slope[...]
        act[t, w] = value.astype(bf16)
        for k in range(7):
            start(pb_copy(t, k))

    for t in range(2):
        for k in reversed(range(7)):
            pb_copy(t, k).wait_recv()
        product = jnp.dot(
            act[t].reshape(128, 768), (w2, w1t)[t][...], preferred_element_type=f32
        ).reshape(8, 16, 1536)
        keep[t] = product

        def to_back(m, j, t=t):
            back[t, m, j] = keep[t, m, 4 * j : 4 * j + 4, :].astype(bf16)

        for m in NEAR_ORDER:
            for j in range(*SPAN[m]):
                to_back(m, j)
            start(rnear_copy(t, m))
        for i in range(7):
            to_back(*DIRECT[i])
            start(rdirect_copy(t, i))
        start(shared_copy(t))
        shared[t, 0] = act[t, :, :, :384]

    for t in range(2):
        for m in reversed(NEAR_ORDER):
            rnear_copy(t, m).wait_recv()
        for j in FAR_ORDER:
            total = keep[t, 0, 4 * j : 4 * j + 4, :]
            for m in NEAR_ORDER:
                if SPAN[m][0] <= j < SPAN[m][1]:
                    total = total + nearrecv[t, m, j].astype(f32)
            farsend[t, j] = total.astype(bf16)
            start(rfar_copy(t, j))

    for t in range(2):
        rows_copy(1 - t).wait_recv()
        shared_copy(t).wait_recv()
        units = shared[t].reshape(256, 384)
        other = rows[1 - t].reshape(256, 1536)
        if t == 0:
            gow[...] = lax.dot_general(
                units, other, (((0,), (0,)), ((), ())), preferred_element_type=f32
            ).astype(bf16)
        else:
            giw[...] = lax.dot_general(
                other, units, (((0,), (0,)), ((), ())), preferred_element_type=f32
            ).astype(bf16)

    for t in range(2):
        total = keep[t, HOME[0], 4 * HOME[1] : 4 * HOME[1] + 4, :]
        for i in range(7):
            rdirect_copy(t, i).wait_recv()
            total = total + directrecv[t, i].astype(f32)
        for j in reversed(FAR_ORDER):
            rfar_copy(t, j).wait_recv()
            total = total + farrecv[t, j].astype(f32)
        (res_ref, gt_ref)[t][...] = total.astype(bf16)

    for copy in sent:
        copy.wait_send()


def store_kernel(res, gt, giw, gow, res_hbm, gt_hbm, giw_hbm, gow_hbm, sem):
    pieces = [(res, res_hbm), (gt, gt_hbm)]
    for i in range(4):
        for src, dst, n in ((giw, giw_hbm, 384), (gow, gow_hbm, 96)):
            pieces.append((src.at[pl.ds(i * n, n)], dst.at[pl.ds(i * n, n)]))
    stores = [pltpu.make_async_copy(*piece, sem.at[i]) for i, piece in enumerate(pieces)]
    for store in stores:
        store.start()
    for store in stores:
        store.wait()


def on_device(*arguments):
    vmem = pl.BlockSpec(memory_space=pltpu.VMEM)
    hbm = pl.BlockSpec(memory_space=pltpu.HBM)
    dma = pltpu.SemaphoreType.DMA
    out_shape = (
        jax.ShapeDtypeStruct((4, 1536), bf16),
        jax.ShapeDtypeStruct((4, 1536), bf16),
        jax.ShapeDtypeStruct((1536, 384), bf16),
        jax.ShapeDtypeStruct((384, 1536), bf16),
    )
    outputs = pl.pallas_call(
        kernel,
        out_shape=out_shape,
        in_specs=[hbm] * 4,
        out_specs=(vmem,) * 4,
        scratch_shapes=[
            pltpu.VMEM((1536, 768), bf16),
            pltpu.VMEM((768, 1536), bf16),
            pltpu.VMEM((768, 1536), bf16),
            pltpu.VMEM((1536, 768), bf16),
            pltpu.VMEM((2, 4, 1536), bf16),
            pltpu.VMEM((2, 8, 4, 4, 1536), bf16),
            pltpu.VMEM((2, 16, 1536), f32),
            pltpu.VMEM((2, 2, 8, 16, 1536), bf16),
            pltpu.VMEM((2, 8, 16, 768), bf16),
            pltpu.VMEM((2, 7, 16, 768), bf16),
            pltpu.VMEM((2, 8, 16, 768), bf16),
            pltpu.VMEM((2, 2, 8, 16, 384), bf16),
            pltpu.VMEM((16, 768), f32),
            pltpu.VMEM((2, 8, 16, 1536), f32),
            pltpu.VMEM((2, 8, 4, 4, 1536), bf16),
            pltpu.VMEM((2, 8, 4, 4, 1536), bf16),
            pltpu.VMEM((2, 7, 4, 1536), bf16),
            pltpu.VMEM((2, 4, 4, 1536), bf16),
            pltpu.VMEM((2, 4, 4, 1536), bf16),
            dma((4,)),
        ]
        + [dma((2,))] * 6
        + [dma((2, n)) for n in (4, 4, 8, 8, 7, 7, 7, 7, 8, 8, 4, 4, 7, 7, 7, 7)],
        compiler_params=pltpu.CompilerParams(
            collective_id=0, has_side_effects=True, vmem_limit_bytes=40 * 2**20
        ),
        cost_estimate=pl.CostEstimate(
            flops=12 * 256 * 1536 * 384, bytes_accessed=4 * 1536 * 384 * 2, transcendentals=32 * 384
        ),
    )(*(pltpu.with_memory_space_constraint(a, pltpu.HBM) for a in arguments))
    return pl.pallas_call(
        store_kernel,
        out_shape=out_shape,
        in_specs=[vmem] * 4,
        out_specs=(hbm,) * 4,
        scratch_shapes=[dma((10,))],
        compiler_params=pltpu.CompilerParams(vmem_limit_bytes=8 * 2**20),
    )(*outputs)


def solution(mesh):
    in_specs = (
        P(("inp", "out"), "wgt"),
        P("wgt", ("inp", "out")),
        P(("inp", "out"), "wgt"),
        P(("inp", "out"), "wgt"),
    )
    out_specs = (
        P(("inp", "out"), "wgt"),
        P(("inp", "out"), "wgt"),
        P("wgt", ("inp", "out")),
        P(("inp", "out"), "wgt"),
    )
    return jax.shard_map(
        on_device, mesh=mesh, in_specs=in_specs, out_specs=out_specs, check_vma=False
    )
```

```python
import math

import jax
import jax.numpy as jnp
from jax import lax
from jax.experimental import pallas as pl
from jax.experimental.pallas import tpu as pltpu
from jax.sharding import PartitionSpec as P

MESH = pl.DeviceIdType.MESH
f32 = jnp.float32
bf16 = jnp.bfloat16

gelu_c = math.sqrt(2.0 / math.pi)

FAR = (-2, -6, 6, 2)
FAR_ORDER = (1, 2, 0, 3)
NEAR = ((0, 0), (1, 0), (-1, 0), (2, 0), (0, 1), (1, 1), (-1, 1), (-2, 1))
NEAR_ORDER = (7, 5, 6, 3, 4, 1, 2)
SPAN = (None, (1, 4), (0, 3), (1, 4), (1, 3), (1, 4), (0, 3), (0, 3))
DIRECT = ((4, 0), (4, 3), (5, 0), (6, 3), (1, 0), (2, 3), (7, 3))
HOME = (3, 0)
PEERS = ((2, 1), (1, 1), (3, 1), (2, 0), (0, 1), (1, 0), (3, 0))


def gelu_value_and_slope(v):
    inner = jnp.tanh(gelu_c * (v + 0.044715 * v * v * v))
    value = 0.5 * v * (1.0 + inner)
    slope = 0.5 * (1.0 + inner) + 0.5 * v * (1.0 - inner * inner) * gelu_c * (
        1.0 + 3.0 * 0.044715 * v * v
    )
    return value, slope


def kernel(
    tok_hbm, w1_hbm, w2_hbm, cot_hbm,
    res_ref, gt_ref, giw, gow,
    w1, w2, w1t, w2t,
    own, blocks, stage, rows, part, recva, act, shared, slope,
    keep, back, nearrecv, directrecv, farsend, farrecv,
    load_sem, weight_s, weight_r, rows_s, rows_r, shared_s, shared_r,
    far_s, far_r, near_s, near_r, pa_s, pa_r, pb_s, pb_r,
    rnear_s, rnear_r, rfar_s, rfar_r, direct_s, direct_r, rdirect_s, rdirect_r,
):
    z = lax.axis_index("inp")
    w = lax.axis_index("wgt")
    o = lax.axis_index("out")
    x = w % 4
    yh = w // 4

    mate = o + 1 - 2 * (o % 2)
    sibling = (z, w, mate)

    def at_z(dz, dy=0):
        return ((z + dz + 16) % 16, w, (mate + 2 * dy) % 4)

    def peer_index(k):
        dx, dy = PEERS[k]
        return ((yh + dy) % 2) * 4 + (x + dx) % 4

    loads = [
        pltpu.make_async_copy(src, dst, load_sem.at[i])
        for i, (src, dst) in enumerate(
            (
                (tok_hbm, own.at[0]),
                (cot_hbm, own.at[1]),
                (w2_hbm, w2.at[pl.ds(0, 384)]),
                (w1_hbm, w1.at[:, pl.ds(0, 384)]),
            )
        )
    ]
    for load in loads:
        load.start()

    barrier = pltpu.get_barrier_semaphore()
    partners = [at_z(d) for d in (6, -6, 2, -2, 1, -1)]
    partners += [at_z(d, 1) for d in (2, -2, 1, -1, 0)]
    partners += [(z, peer_index(k), o) for k in range(7)]
    partners += [sibling]
    for partner in partners:
        pl.semaphore_signal(barrier, inc=1, device_id=partner, device_id_type=MESH)
    loads[0].wait()
    loads[1].wait()
    pl.semaphore_wait(barrier, len(partners))

    def remote(src, dst, send, recv, device):
        return pltpu.make_async_remote_copy(
            src_ref=src, dst_ref=dst, send_sem=send, recv_sem=recv,
            device_id=device, device_id_type=MESH,
        )

    sent = []

    def start(copy):
        copy.start()
        sent.append(copy)

    def far_copy(t, j):
        return remote(own.at[t], blocks.at[t, 0, j], far_s.at[t, j], far_r.at[t, j], at_z(-FAR[j]))

    def direct_copy(t, i):
        m, j = DIRECT[i]
        dz, dy = NEAR[m]
        return remote(
            own.at[t], blocks.at[t, m, j], direct_s.at[t, i], direct_r.at[t, i],
            at_z(-dz - FAR[j], dy),
        )

    def near_copy(t, m):
        dz, dy = NEAR[m]
        span = pl.ds(SPAN[m][0], SPAN[m][1] - SPAN[m][0])
        return remote(
            blocks.at[t, 0, span], blocks.at[t, m, span], near_s.at[t, m], near_r.at[t, m],
            at_z(-dz, dy),
        )

    def rows_copy(t):
        return remote(rows.at[t, 0], rows.at[t, 1], rows_s.at[t], rows_r.at[t], sibling)

    def shared_copy(t):
        return remote(
            act.at[t, :, :, pl.ds(384, 384)], shared.at[t, 1], shared_s.at[t], shared_r.at[t],
            sibling,
        )

    def pa_copy(t, k):
        p = peer_index(k)
        return remote(part.at[t, p], recva.at[t, k], pa_s.at[t, k], pa_r.at[t, k], (z, p, o))

    def pb_copy(t, k):
        return remote(
            act.at[t, w], act.at[t, w], pb_s.at[t, k], pb_r.at[t, k], (z, peer_index(k), o)
        )

    def rdirect_copy(t, i):
        m, j = DIRECT[i]
        dz, dy = NEAR[m]
        return remote(
            back.at[t, m, j], directrecv.at[t, i], rdirect_s.at[t, i], rdirect_r.at[t, i],
            at_z(dz + FAR[j], dy),
        )

    def rnear_copy(t, m):
        dz, dy = NEAR[m]
        span = pl.ds(SPAN[m][0], SPAN[m][1] - SPAN[m][0])
        return remote(
            back.at[t, m, span], nearrecv.at[t, m, span], rnear_s.at[t, m], rnear_r.at[t, m],
            at_z(dz, dy),
        )

    def rfar_copy(t, j):
        return remote(
            farsend.at[t, j], farrecv.at[t, j], rfar_s.at[t, j], rfar_r.at[t, j], at_z(FAR[j])
        )

    for t in range(2):
        for j in FAR_ORDER:
            start(far_copy(t, j))
    for t in range(2):
        for i in range(7):
            start(direct_copy(t, i))
    weights = (
        remote(w2_hbm, w2.at[pl.ds(384, 384)], weight_s.at[0], weight_r.at[0], sibling),
        remote(w1_hbm, w1.at[:, pl.ds(384, 384)], weight_s.at[1], weight_r.at[1], sibling),
    )
    for copy in weights:
        start(copy)
    for t in range(2):
        blocks[t, HOME[0], HOME[1]] = own[t]
    loads[2].wait()
    weights[0].wait_recv()
    w2t[...] = w2[...].T

    def to_rows(t, m):
        for j in range(4):
            stage[t, 4 * j : 4 * j + 4, :] = blocks[t, m, j].astype(f32)
        rows[t, 0, m] = stage[t].astype(bf16)

    for t in range(2):
        for j in reversed(FAR_ORDER):
            far_copy(t, j).wait_recv()
        for m in NEAR_ORDER:
            start(near_copy(t, m))
        to_rows(t, 0)
    loads[3].wait()
    weights[1].wait_recv()
    w1t[...] = w1[...].T

    for t in range(2):
        for i in range(7):
            direct_copy(t, i).wait_recv()
        for m in reversed(NEAR_ORDER):
            near_copy(t, m).wait_recv()
            to_rows(t, m)
        part[t] = (
            jnp.dot(
                rows[t, 0].reshape(128, 1536), (w1, w2t)[t][...], preferred_element_type=f32
            )
            .astype(bf16)
            .reshape(8, 16, 768)
        )
        for k in range(7):
            start(pa_copy(t, k))
        start(rows_copy(t))

    for t in range(2):
        total = part[t, w].astype(f32)
        for k in reversed(range(7)):
            pa_copy(t, k).wait_recv()
            total = total + recva[t, k].astype(f32)
        if t == 0:
            value, slope_value = gelu_value_and_slope(total)
            slope[...] = slope_value
        else:
            value = total * slope[...]
        act[t, w] = value.astype(bf16)
        for k in range(7):
            start(pb_copy(t, k))

    for t in range(2):
        for k in reversed(range(7)):
            pb_copy(t, k).wait_recv()
        product = jnp.dot(
            act[t].reshape(128, 768), (w2, w1t)[t][...], preferred_element_type=f32
        ).reshape(8, 16, 1536)
        keep[t] = product

        def to_back(m, j, t=t):
            back[t, m, j] = keep[t, m, 4 * j : 4 * j + 4, :].astype(bf16)

        for m in NEAR_ORDER:
            for j in range(*SPAN[m]):
                to_back(m, j)
            start(rnear_copy(t, m))
        for i in range(7):
            to_back(*DIRECT[i])
            start(rdirect_copy(t, i))
        start(shared_copy(t))
        shared[t, 0] = act[t, :, :, :384]

    for t in range(2):
        for m in reversed(NEAR_ORDER):
            rnear_copy(t, m).wait_recv()
        for j in FAR_ORDER:
            total = keep[t, 0, 4 * j : 4 * j + 4, :]
            for m in NEAR_ORDER:
                if SPAN[m][0] <= j < SPAN[m][1]:
                    total = total + nearrecv[t, m, j].astype(f32)
            farsend[t, j] = total.astype(bf16)
            start(rfar_copy(t, j))

    for t in range(2):
        rows_copy(1 - t).wait_recv()
        shared_copy(t).wait_recv()
        units = shared[t].reshape(256, 384)
        other = rows[1 - t].reshape(256, 1536)
        if t == 0:
            gow[...] = lax.dot_general(
                units, other, (((0,), (0,)), ((), ())), preferred_element_type=f32
            ).astype(bf16)
        else:
            giw[...] = lax.dot_general(
                other, units, (((0,), (0,)), ((), ())), preferred_element_type=f32
            ).astype(bf16)

    for t in range(2):
        total = keep[t, HOME[0], 4 * HOME[1] : 4 * HOME[1] + 4, :]
        for i in range(7):
            rdirect_copy(t, i).wait_recv()
            total = total + directrecv[t, i].astype(f32)
        for j in reversed(FAR_ORDER):
            rfar_copy(t, j).wait_recv()
            total = total + farrecv[t, j].astype(f32)
        (res_ref, gt_ref)[t][...] = total.astype(bf16)

    for copy in sent:
        copy.wait_send()


def store_kernel(res, gt, giw, gow, res_hbm, gt_hbm, giw_hbm, gow_hbm, sem):
    pieces = [(res, res_hbm), (gt, gt_hbm)]
    for i in range(4):
        for src, dst, n in ((giw, giw_hbm, 384), (gow, gow_hbm, 96)):
            pieces.append((src.at[pl.ds(i * n, n)], dst.at[pl.ds(i * n, n)]))
    stores = [pltpu.make_async_copy(*piece, sem.at[i]) for i, piece in enumerate(pieces)]
    for store in stores:
        store.start()
    for store in stores:
        store.wait()


def on_device(*arguments):
    vmem = pl.BlockSpec(memory_space=pltpu.VMEM)
    hbm = pl.BlockSpec(memory_space=pltpu.HBM)
    dma = pltpu.SemaphoreType.DMA
    out_shape = (
        jax.ShapeDtypeStruct((4, 1536), bf16),
        jax.ShapeDtypeStruct((4, 1536), bf16),
        jax.ShapeDtypeStruct((1536, 384), bf16),
        jax.ShapeDtypeStruct((384, 1536), bf16),
    )
    outputs = pl.pallas_call(
        kernel,
        out_shape=out_shape,
        in_specs=[hbm] * 4,
        out_specs=(vmem,) * 4,
        scratch_shapes=[
            pltpu.VMEM((1536, 768), bf16),
            pltpu.VMEM((768, 1536), bf16),
            pltpu.VMEM((768, 1536), bf16),
            pltpu.VMEM((1536, 768), bf16),
            pltpu.VMEM((2, 4, 1536), bf16),
            pltpu.VMEM((2, 8, 4, 4, 1536), bf16),
            pltpu.VMEM((2, 16, 1536), f32),
            pltpu.VMEM((2, 2, 8, 16, 1536), bf16),
            pltpu.VMEM((2, 8, 16, 768), bf16),
            pltpu.VMEM((2, 7, 16, 768), bf16),
            pltpu.VMEM((2, 8, 16, 768), bf16),
            pltpu.VMEM((2, 2, 8, 16, 384), bf16),
            pltpu.VMEM((16, 768), f32),
            pltpu.VMEM((2, 8, 16, 1536), f32),
            pltpu.VMEM((2, 8, 4, 4, 1536), bf16),
            pltpu.VMEM((2, 8, 4, 4, 1536), bf16),
            pltpu.VMEM((2, 7, 4, 1536), bf16),
            pltpu.VMEM((2, 4, 4, 1536), bf16),
            pltpu.VMEM((2, 4, 4, 1536), bf16),
            dma((4,)),
        ]
        + [dma((2,))] * 6
        + [dma((2, n)) for n in (4, 4, 8, 8, 7, 7, 7, 7, 8, 8, 4, 4, 7, 7, 7, 7)],
        compiler_params=pltpu.CompilerParams(
            collective_id=0, has_side_effects=True, vmem_limit_bytes=40 * 2**20
        ),
        cost_estimate=pl.CostEstimate(
            flops=12 * 256 * 1536 * 384, bytes_accessed=4 * 1536 * 384 * 2, transcendentals=32 * 384
        ),
    )(*(pltpu.with_memory_space_constraint(a, pltpu.HBM) for a in arguments))
    return pl.pallas_call(
        store_kernel,
        out_shape=out_shape,
        in_specs=[vmem] * 4,
        out_specs=(hbm,) * 4,
        scratch_shapes=[dma((10,))],
        compiler_params=pltpu.CompilerParams(vmem_limit_bytes=8 * 2**20),
    )(*outputs)


def solution(mesh):
    in_specs = (
        P(("inp", "out"), "wgt"),
        P("wgt", ("inp", "out")),
        P(("inp", "out"), "wgt"),
        P(("inp", "out"), "wgt"),
    )
    out_specs = (
        P(("inp", "out"), "wgt"),
        P(("inp", "out"), "wgt"),
        P("wgt", ("inp", "out")),
        P(("inp", "out"), "wgt"),
    )
    return jax.shard_map(
        on_device, mesh=mesh, in_specs=in_specs, out_specs=out_specs, check_vma=False
    )
```
